32 devices in a mesh: ep: 16 (over z, x, core), tp: 2 (over y).
Axes of the slice: x: 2, y: 2, z: 4, core: 2. Of those that a mesh axis runs over, the one named last changes fastest.
Arguments:
- attn_out: bfloat16 [2048, 2048], P('ep', 'tp'), may hold values from -6 to 6
- resid: bfloat16 [2048, 2048], P(('ep', 'tp')), may hold values from -6 to 6
- norm_gain: float32 [2048], replicated, may hold values from 0.1 to 1.9
- expert_ids: int32 [2048, 6], P('ep'), may hold values from 0 to 15, all different within a row; in each aligned block of 128 rows (0 to 127, 128 to 255, ...) at most 64 rows name the same one
- gate_vals: float32 [2048, 6], P('ep'), may hold values from 0.1 to 1
- w_gate: bfloat16 [16, 1408, 2048], P('ep', 'tp'), may hold values from -0.125 to 0.125
- w_up: bfloat16 [16, 1408, 2048], P('ep', 'tp'), may hold values from -0.125 to 0.125
- w_down: bfloat16 [16, 1408, 2048], P('ep', 'tp'), may hold values from -0.15625 to 0.15625
Outputs:
- layer_out: bfloat16 [2048, 2048], P(('ep', 'tp'))
The draws below stay inside these ranges and needn't reach their ends.
Inputs may be any that keep to these rules, and one draw needn't show every extreme that they name: `expert_ids`: among the tokens of one index of ep (aligned blocks of 128 rows), no expert is chosen by more than 64 tokens; some expert reaches 64 in some blocks. The experts of one token differ.
All inputs are finite; a program needn't handle non-finite values.
Results may differ from the reference program's by a relative error of at most 0.0095.
Values may be sent and summed in bfloat16 or wider, within the bound.
No kernel may reach another device: no remote copies, remote signals or barrier semaphores. Data moves between devices by JAX's collectives and lax.ppermute only.
A program may use at most 64 MiB of HBM per device.

```python
import math
import jax
import jax.numpy as jnp
import numpy as np
from jax import lax

D = 2048
FF = 1408
TOP = 6
TOK_EP = 128
EXPERTS = 16
TOKENS = 2048
CAP = 64
FF_DEV = 704
N_EP = 16
N_TP = 2


def block_levels(stream_key, extent, pieces, low, high):
    loudness, own = 1.0, jax.random.fold_in(stream_key, 6)
    for dim, parts in pieces:
        steps = jnp.exp(jax.random.uniform(jax.random.fold_in(own, dim), (parts,), jnp.float32, low / len(pieces), high / len(pieces)))
        loudness = loudness * jnp.repeat(steps, extent[dim] // parts).reshape([-1 if axis == dim else 1 for axis in range(len(extent))])
    return loudness


def shared_out(stream_key, own, number, rows, number_of, top, bound, skew):
    ranking = jax.random.permutation(stream_key, number_of)
    packed, usual = shares(number_of, rows * top, bound, skew, True), shares(number_of, rows * top, bound, skew, False)
    places = jnp.arange(number_of)

    def named(lengths, rotation):
        used = int((lengths > 0).sum())
        fixed = max(1, used // 4)
        passed = fixed + (places - fixed + rotation * (used - fixed)) % max(1, number_of - fixed)
        return jnp.zeros((number_of,), jnp.int32).at[ranking[jnp.where(places < fixed, places, passed)]].set(jnp.asarray(lengths, jnp.int32))

    lengths = jnp.where(number % 4 == 0, named(packed, number // 4), named(usual, number - number // 4 - 1))
    mixed = jax.random.permutation(jax.random.fold_in(own, 3), number_of)
    donor, sink = mixed[0:number_of // 2 * 2:2], mixed[1:number_of // 2 * 2:2]
    margin = jnp.minimum(lengths[donor] - 1, bound - lengths[sink]) // 2
    margin = jnp.where((donor == ranking[0]) | (sink == ranking[0]) | (lengths[sink] == 0), 0, jnp.maximum(margin, 0))
    passed = jax.random.randint(jax.random.fold_in(own, 4), (number_of // 2,), 0, 1 << 20) % (margin + 1)
    lengths = lengths.at[donor].add(-passed).at[sink].add(passed)
    labels = jnp.searchsorted(jnp.cumsum(lengths), jnp.arange(rows * top), side="right").astype(jnp.int32)
    table = labels.reshape(top, rows).T
    table = table[jax.random.permutation(jax.random.fold_in(own, 1), rows)]
    rotation = jax.random.randint(jax.random.fold_in(own, 2), (rows, 1), 0, top)
    return jnp.take_along_axis(table, (jnp.arange(top)[None, :] + rotation) % top, axis=1)


def shares(count, total, bound, slope, full):
    loads = [(1 << 20) // math.isqrt(standing ** slope) + 1 for standing in range(1, count + 1)]
    largest = bound if full else min(bound, max(-(-total // count), total * loads[0] // sum(loads)))
    least = 1 if total - largest >= count - 1 else 0
    counts, surplus = [largest] + [least] * (count - 1), total - largest - least * (count - 1)
    while surplus > 0:
        movable = [i for i in range(1, count) if counts[i] < largest] or [i for i in range(1, count) if counts[i] < bound]
        whole, remaining = sum([loads[i] for i in movable]), surplus
        for i in movable:
            addition = min(bound - counts[i], max(1, remaining * loads[i] // whole), surplus)
            counts[i] = counts[i] + addition
            surplus = surplus - addition
    return np.array(counts)


def bell_draw(stream_key, shape, width, most, shards=(), kind=jnp.bfloat16):
    result = width * jax.random.normal(stream_key, shape, jnp.float32)
    if shards:
        result = result * block_levels(stream_key, shape, shards, -0.22, 0.18)
    return jnp.clip(result, -most, most).astype(kind)


def setup_inputs(seed: int = 0) -> dict:
    key_list = jax.random.split(jax.random.key(seed), 9)
    attn_out = bell_draw(key_list[0], (TOKENS, D), 1.0, 6.0, ((0, 16), (1, 2)))
    resid = bell_draw(key_list[1], (TOKENS, D), 1.0, 6.0, ((0, 32),))
    norm_gain = jnp.clip(1.0 + 0.18 * jax.random.normal(key_list[2], (D,), jnp.float32), 0.1, 1.9)
    expert_ids_keys = jax.random.split(jax.random.fold_in(key_list[3], 1), TOKENS // TOK_EP)
    expert_ids_turns = jax.random.permutation(jax.random.fold_in(key_list[3], 3), TOKENS // TOK_EP)
    expert_ids = jax.vmap(lambda own, number: shared_out(jax.random.fold_in(key_list[3], 2), own, number, TOK_EP, EXPERTS, TOP, CAP, 1))(expert_ids_keys, expert_ids_turns).reshape((TOKENS, TOP))
    gate_vals = jnp.clip(jnp.exp(math.log(1.0) - 2.3025851 * jax.random.uniform(key_list[4], (TOKENS, TOP), jnp.float32) ** block_levels(key_list[4], (TOKENS, TOP), ((0, 16),), -0.2, 0.2)), 0.1, 1.0)
    w_gate = bell_draw(key_list[5], (EXPERTS, FF, D), D ** -0.5, 0.125, ((0, 16), (1, 2)))
    w_up = bell_draw(key_list[6], (EXPERTS, FF, D), D ** -0.5, 0.125, ((0, 16), (1, 2)))
    w_down = bell_draw(key_list[7], (EXPERTS, FF, D), FF ** -0.5, 0.15625, ((0, 16), (1, 2)))
    return dict(attn_out=attn_out, resid=resid, norm_gain=norm_gain, expert_ids=expert_ids, gate_vals=gate_vals, w_gate=w_gate, w_up=w_up, w_down=w_down)


def reference(attn_out, resid, norm_gain, expert_ids, gate_vals, w_gate, w_up, w_down):
    hidden_state = (resid.astype(jnp.float32) + attn_out.astype(jnp.float32)).astype(jnp.bfloat16)
    hidden_f32 = hidden_state.astype(jnp.float32)
    mean_sq = lax.optimization_barrier(jnp.mean(hidden_f32 * hidden_f32, axis=-1, keepdims=True))
    normed = (hidden_f32 * lax.rsqrt(mean_sq + 1e-05) * norm_gain.astype(jnp.float32)).astype(jnp.bfloat16)
    pairs = TOK_EP * TOP
    group_ids = expert_ids.reshape(N_EP, pairs).astype(jnp.int32)
    onehot = (group_ids[:, :, None] == jnp.arange(EXPERTS, dtype=jnp.int32)[None, None, :]).astype(jnp.int32)
    rank_in = lax.optimization_barrier(jnp.sum(onehot * (jnp.cumsum(onehot, axis=1) - onehot), axis=-1)).astype(jnp.int32)
    source = jnp.broadcast_to(jnp.arange(N_EP, dtype=jnp.int32)[:, None], (N_EP, pairs))
    token_of = (jnp.arange(N_EP, dtype=jnp.int32)[:, None] * TOK_EP + jnp.arange(pairs, dtype=jnp.int32)[None, :] // TOP).astype(jnp.int32)
    position = ((group_ids * N_EP + source) * CAP + rank_in).reshape(-1)
    table = jnp.full((EXPERTS * N_EP * CAP,), TOKENS, jnp.int32).at[position].set(token_of.reshape(-1))
    weight_table = jnp.zeros((EXPERTS * N_EP * CAP,), jnp.float32).at[position].set(gate_vals.reshape(-1).astype(jnp.float32))
    table = table.reshape(EXPERTS, N_EP * CAP)
    weight_table = weight_table.reshape(EXPERTS, N_EP * CAP)
    padded = jnp.concatenate([normed, jnp.zeros((1, D), jnp.bfloat16)], axis=0)

    def per_expert(carry, items):
        rows_idx, weights, gate_w, up_w, down_w = items
        rows = padded[rows_idx]
        gate_pre = jnp.dot(rows, gate_w.T, preferred_element_type=jnp.float32)
        up_pre = jnp.dot(rows, up_w.T, preferred_element_type=jnp.float32)
        act = (jax.nn.silu(gate_pre) * up_pre).astype(jnp.bfloat16)
        total = jnp.zeros((rows.shape[0], D), jnp.float32)
        for group in range(N_TP):
            part = jnp.dot(act[:, group * FF_DEV:(group + 1) * FF_DEV], down_w[group * FF_DEV:(group + 1) * FF_DEV], preferred_element_type=jnp.float32).astype(jnp.bfloat16)
            total = total + lax.optimization_barrier(part).astype(jnp.float32)
        slot_out = lax.optimization_barrier(total.astype(jnp.bfloat16)).astype(jnp.float32)
        carry = carry.at[rows_idx].add(weights[:, None] * slot_out)
        return (carry, None)
    moe, _ = lax.scan(per_expert, jnp.zeros((TOKENS + 1, D), jnp.float32), (table, weight_table, w_gate, w_up, w_down))
    return (hidden_f32 + moe[:TOKENS]).astype(jnp.bfloat16)
```

```python
import jax
import jax.numpy as jnp
from jax import lax
from jax.sharding import PartitionSpec as P

F32 = jnp.float32
BF16 = jnp.bfloat16
AXES = ("ep", "tp")


def by_feature(rows, weight):
    return lax.dot_general(rows, weight, (((1,), (1,)), ((), ())), preferred_element_type=F32)


def flip_if(odd, a, axis):
    return jnp.where(odd == 1, jnp.flip(a, axis), a)


def norm_rows(attn_out, resid, norm_gain):
    seq_rows = lax.all_to_all(attn_out, "tp", split_axis=0, concat_axis=1, tiled=True)
    hidden_state = (resid.astype(F32) + seq_rows.astype(F32)).astype(BF16)
    hidden_f32 = hidden_state.astype(F32)
    mean_sq = jnp.mean(hidden_f32 * hidden_f32, axis=-1, keepdims=True)
    normed = (hidden_f32 * lax.rsqrt(mean_sq + 1e-05) * norm_gain).astype(BF16)
    return hidden_f32, normed


def expert_rows(rows, w_gate, w_up, w_down):
    gate_pre = by_feature(rows, w_gate)
    up_pre = by_feature(rows, w_up)
    act = (jax.nn.silu(gate_pre) * up_pre).astype(BF16)
    return jnp.dot(act, w_down, preferred_element_type=F32)


def gathered_plan(ep_count, attn_out, resid, norm_gain, expert_ids, gate_vals, w_gate, w_up, w_down):
    planes = ep_count // 4
    me = lax.axis_index("ep")
    core, pair, plane = me % 2, (me // 2) % 2, me // 4
    half = lax.axis_index("tp")

    def routes(move):
        pairs = []
        for e in range(ep_count):
            for t in range(2):
                z, x, c, y = move(e // 4, (e // 2) % 2, e % 2, t)
                pairs.append((e * 2 + t, ((z * 2 + x) * 2 + c) * 2 + y))
        return lambda a: lax.ppermute(a, AXES, pairs)

    first = routes(lambda z, x, c, y: (z, x, c, 1 - y) if c else (z, 1 - x, c, y))
    second = routes(lambda z, x, c, y: (z, 1 - x, c, y) if c else (z, x, c, 1 - y))
    sibling = routes(lambda z, x, c, y: (z, x, 1 - c, y))
    down = routes(lambda z, x, c, y: ((z - 1) % planes, x, c, y))

    top = expert_ids.shape[1]
    table = jnp.stack([expert_ids.T.astype(F32), gate_vals.T])
    table = lax.all_gather(table, "ep", axis=0, tiled=False)
    weight = jnp.sum(jnp.where(table[:, 0] == me.astype(F32), table[:, 1], 0.0), axis=1)
    weight = weight.reshape(planes, 2, 2, 2, -1)
    weight = jnp.moveaxis(weight, 2, 1)
    weight = flip_if(core, weight, 1)
    weight = flip_if(pair, weight, 2)
    weight = flip_if(half, weight, 3)
    pair_major, half_major = weight, jnp.swapaxes(weight, 2, 3)
    own_weight = jnp.where(core == 1, pair_major[:, 0], half_major[:, 0]).reshape(planes, -1)
    sib_weight = jnp.where(core == 1, half_major[:, 1], pair_major[:, 1]).reshape(planes, -1)

    hidden_f32, normed = norm_rows(attn_out, resid, norm_gain)
    my_rows = normed.shape[0]
    slots = 2 * my_rows

    def gather_plane(piece):
        two = jnp.concatenate([piece, first(piece)], axis=0)
        own = jnp.concatenate([two, second(two)], axis=0)
        return own, sibling(own)

    def placing(row_weight):
        chosen = row_weight != 0
        counts = chosen.astype(jnp.int32)
        rank = jnp.cumsum(counts) - counts
        slot = jnp.where(chosen, rank, -1)
        return slot[None, :] == jnp.arange(slots, dtype=jnp.int32)[:, None]

    def experts(own, sib, w_own, w_sib):
        place_own, place_sib = placing(w_own), placing(w_sib)
        rows = jnp.concatenate(
            [
                jnp.dot(place_own.astype(BF16), own, preferred_element_type=F32).astype(BF16),
                jnp.dot(place_sib.astype(BF16), sib, preferred_element_type=F32).astype(BF16),
            ],
            axis=0,
        )
        scale = jnp.concatenate(
            [
                jnp.sum(jnp.where(place_own, w_own[None, :], 0.0), axis=1),
                jnp.sum(jnp.where(place_sib, w_sib[None, :], 0.0), axis=1),
            ]
        )
        out = (expert_rows(rows, w_gate[0], w_up[0], w_down[0]) * scale[:, None]).astype(BF16)

        def back(place, slot_rows):
            return lax.dot_general(
                place.astype(BF16), slot_rows, (((0,), (0,)), ((), ())), preferred_element_type=F32
            ).astype(BF16)

        return back(place_own, out[:slots]), back(place_sib, out[slots:])

    def add(a, b):
        return (a.astype(F32) + b.astype(F32)).astype(BF16)

    pieces = [normed]
    for _ in range(planes - 1):
        pieces.append(down(pieces[-1]))
    gathered = [gather_plane(piece) for piece in pieces]
    carried = None
    for step in list(range(1, planes)) + [0]:
        source = (plane + step) % planes
        w_own = lax.dynamic_index_in_dim(own_weight, source, 0, keepdims=False)
        w_sib = lax.dynamic_index_in_dim(sib_weight, source, 0, keepdims=False)
        out_own, out_sib = experts(*gathered[step], w_own, w_sib)
        total = add(out_own, sibling(out_sib))
        kept = total[:slots].astype(F32) + second(total[slots:]).astype(F32)
        if carried is not None:
            kept = kept + carried.astype(F32)
        kept = kept.astype(BF16)
        if step:
            carried = down(kept)
    moe_rows = kept[:my_rows].astype(F32) + first(kept[my_rows:]).astype(F32)
    return (hidden_f32 + moe_rows).astype(BF16)


def exchanged_plan(ep_count, attn_out, resid, norm_gain, expert_ids, gate_vals, w_gate, w_up, w_down):
    hidden_f32, normed = norm_rows(attn_out, resid, norm_gain)
    normed_all = lax.all_gather(normed, "tp", axis=0, tiled=True)
    tok_block, width = normed_all.shape
    capacity = 4 * tok_block * expert_ids.shape[1] // (3 * ep_count)
    flat_ids = expert_ids.reshape(-1)
    onehot = (flat_ids[:, None] == jnp.arange(ep_count, dtype=jnp.int32)[None, :]).astype(jnp.int32)
    rank_in = jnp.sum(onehot * (jnp.cumsum(onehot, axis=0) - onehot), axis=1)
    slot_index = (flat_ids * capacity + rank_in).reshape(tok_block, -1)
    slot_range = jnp.arange(ep_count * capacity, dtype=jnp.int32)
    hit = slot_index[None, :, :] == slot_range[:, None, None]
    placing = jnp.any(hit, axis=-1).astype(BF16)
    send_rows = jnp.dot(placing, normed_all, preferred_element_type=F32).astype(BF16)
    send_rows = send_rows.reshape(ep_count, capacity, width)
    received = lax.all_to_all(send_rows, "ep", split_axis=0, concat_axis=0, tiled=True)
    out_rows = expert_rows(received.reshape(-1, width), w_gate[0], w_up[0], w_down[0]).astype(BF16)
    back_rows = lax.all_to_all(
        out_rows.reshape(received.shape), "ep", split_axis=0, concat_axis=0, tiled=True
    )
    scale = jnp.sum(jnp.where(hit, gate_vals[None, :, :], 0.0), axis=(1, 2))
    weighted = (back_rows.reshape(-1, width).astype(F32) * scale[:, None]).astype(BF16)
    part = lax.dot_general(placing, weighted, (((0,), (0,)), ((), ())), preferred_element_type=F32)
    moe_rows = lax.psum_scatter(part, "tp", scatter_dimension=0, tiled=True)
    return (hidden_f32 + moe_rows).astype(BF16)


def solution(mesh):
    ep_count, tp_count = mesh.shape["ep"], mesh.shape["tp"]
    plan = gathered_plan if tp_count == 2 and ep_count % 4 == 0 else exchanged_plan

    def per_device(*arguments):
        return plan(ep_count, *arguments)

    in_specs = (
        P("ep", "tp"),
        P(AXES, None),
        P(),
        P("ep", None),
        P("ep", None),
        P("ep", "tp", None),
        P("ep", "tp", None),
        P("ep", "tp", None),
    )
    return jax.shard_map(
        per_device, mesh=mesh, in_specs=in_specs, out_specs=P(AXES, None), check_vma=False
    )
```

```python
import functools

import jax
import jax.numpy as jnp
from jax import lax
from jax.experimental import pallas as pl
from jax.experimental.pallas import tpu as pltpu
from jax.sharding import PartitionSpec as P

F32 = jnp.float32
BF16 = jnp.bfloat16
AXES = ("ep", "tp")
LANES = 128
VMEM = pl.BlockSpec(memory_space=pltpu.VMEM)
SMEM = pl.BlockSpec(memory_space=pltpu.SMEM)


def by_feature(rows, weight):
    return lax.dot_general(rows, weight, (((1,), (1,)), ((), ())), preferred_element_type=F32)


def norm_rows(attn_out, resid, norm_gain):
    seq_rows = lax.all_to_all(attn_out, "tp", split_axis=0, concat_axis=1, tiled=True)
    hidden_state = (resid.astype(F32) + seq_rows.astype(F32)).astype(BF16)
    hidden_f32 = hidden_state.astype(F32)
    mean_sq = jnp.mean(hidden_f32 * hidden_f32, axis=-1, keepdims=True)
    normed = (hidden_f32 * lax.rsqrt(mean_sq + 1e-05) * norm_gain).astype(BF16)
    return hidden_f32, normed


def expert_rows(rows, w_gate, w_up, w_down):
    gate_pre = by_feature(rows, w_gate)
    up_pre = by_feature(rows, w_up)
    act = (jax.nn.silu(gate_pre) * up_pre).astype(BF16)
    return jnp.dot(act, w_down, preferred_element_type=F32)


def tiles(extent, size):
    return [(start, min(size, extent - start)) for start in range(0, extent, size)]


def product(a, b, a_dim, b_dim):
    return lax.dot_general(a, b, (((a_dim,), (b_dim,)), ((), ())), preferred_element_type=F32)


def front_kernel(cols_ref, resid_ref, gain_ref, ids_ref, gates_ref, packed_ref, hidden_ref):
    shares, rows, columns = cols_ref.shape
    width = resid_ref.shape[1]
    attn = jnp.concatenate([cols_ref[i] for i in range(shares)], axis=1)
    hidden_state = (resid_ref[...].astype(F32) + attn.astype(F32)).astype(BF16)
    hidden_ref[...] = hidden_state
    hidden = hidden_state.astype(F32)
    mean_sq = jnp.mean(hidden * hidden, axis=1, keepdims=True)
    packed_ref[:, :width] = (hidden * lax.rsqrt(mean_sq + 1e-05) * gain_ref[...]).astype(BF16)
    lane = lax.broadcasted_iota(jnp.int32, (rows, LANES), 1)
    weight = jnp.zeros((rows, LANES), F32)
    for k in range(ids_ref.shape[1]):
        hit = lane % (LANES // 2) == ids_ref[:, k : k + 1]
        weight = weight + jnp.where(hit, gates_ref[:, k : k + 1], 0.0)
    high = weight.astype(BF16).astype(F32)
    packed_ref[:, width:] = jnp.where(lane < LANES // 2, high, weight - high).astype(BF16)


def front(cols, resid, norm_gain, ids, gates):
    rows, width = resid.shape
    return pl.pallas_call(
        front_kernel,
        out_shape=(
            jax.ShapeDtypeStruct((rows, width + LANES), BF16),
            jax.ShapeDtypeStruct((rows, width), BF16),
        ),
        in_specs=[VMEM] * 5,
        out_specs=(VMEM, VMEM),
        compiler_params=pltpu.CompilerParams(vmem_limit_bytes=8 * 2**20),
    )(cols, resid, norm_gain.reshape(1, -1), ids, gates)


def expert_kernel(me_ref, own_ref, sib_ref, gate_ref, up_ref, down_ref, own_out, sib_out, rows, act):
    count = own_ref.shape[0]
    hidden_units, width = down_ref.shape
    slots = count // 2
    me = me_ref[0]
    row = lax.broadcasted_iota(jnp.int32, (count, count), 0)
    column = lax.broadcasted_iota(jnp.int32, (count, count), 1)
    earlier = jnp.where(column < row, 1.0, 0.0).astype(BF16)
    slot = lax.broadcasted_iota(jnp.int32, (count, slots), 1).astype(F32)

    def placing(source):
        routing = source[:, width:].astype(F32)
        lane = lax.broadcasted_iota(jnp.int32, routing.shape, 1)
        weight = jnp.sum(jnp.where(lane % (LANES // 2) == me, routing, 0.0), axis=1, keepdims=True)
        chosen = jnp.broadcast_to(jnp.where(weight != 0, 1.0, 0.0), (count, slots))
        rank = product(earlier, chosen.astype(BF16), 1, 0)
        return jnp.where(rank == slot, chosen, 0.0).astype(BF16), weight

    place_own, weight_own = placing(own_ref)
    place_sib, weight_sib = placing(sib_ref)
    for start, size in tiles(width, 512):
        part = slice(start, start + size)
        rows[:slots, part] = product(place_own, own_ref[:, part], 0, 0).astype(BF16)
        rows[slots:, part] = product(place_sib, sib_ref[:, part], 0, 0).astype(BF16)
    for start, size in tiles(hidden_units, 256):
        part = slice(start, start + size)
        gate_pre = product(rows[...], gate_ref[part, :], 1, 1)
        up_pre = product(rows[...], up_ref[part, :], 1, 1)
        act[:, part] = (gate_pre / (1.0 + jnp.exp(-gate_pre)) * up_pre).astype(BF16)
    for start, size in tiles(width, 1024):
        part = slice(start, start + size)
        out = product(act[...], down_ref[:, part], 1, 0).astype(BF16)
        own_out[:, part] = (product(place_own, out[:slots], 1, 0) * weight_own).astype(BF16)
        sib_out[:, part] = (product(place_sib, out[slots:], 1, 0) * weight_sib).astype(BF16)


def experts(me, own, sib, w_gate, w_up, w_down):
    count = own.shape[0]
    hidden_units, width = w_down.shape
    result = jax.ShapeDtypeStruct((count, width), BF16)
    return pl.pallas_call(
        expert_kernel,
        out_shape=(result, result),
        in_specs=[SMEM] + [VMEM] * 5,
        out_specs=(VMEM, VMEM),
        scratch_shapes=[pltpu.VMEM((count, width), BF16), pltpu.VMEM((count, hidden_units), BF16)],
        compiler_params=pltpu.CompilerParams(vmem_limit_bytes=30 * 2**20),
        cost_estimate=pl.CostEstimate(
            flops=6 * count * width * hidden_units, bytes_accessed=8 * count * width, transcendentals=0
        ),
    )(me, own, sib, w_gate, w_up, w_down)


def gathered_plan(ep_count, attn_out, resid, norm_gain, expert_ids, gate_vals, w_gate, w_up, w_down):
    planes = ep_count // 4
    my_rows = resid.shape[0]
    half = lax.axis_index("tp")

    def routes(move):
        pairs = []
        for e in range(ep_count):
            for t in range(2):
                z, x, c, y = move(e // 4, (e // 2) % 2, e % 2, t)
                pairs.append((e * 2 + t, ((z * 2 + x) * 2 + c) * 2 + y))
        return lambda a: lax.ppermute(a, AXES, pairs)

    first = routes(lambda z, x, c, y: (z, x, c, 1 - y) if c else (z, 1 - x, c, y))
    second = routes(lambda z, x, c, y: (z, 1 - x, c, y) if c else (z, x, c, 1 - y))
    sibling = routes(lambda z, x, c, y: (z, x, 1 - c, y))
    down = routes(lambda z, x, c, y: ((z - 1) % planes, x, c, y))

    cols = attn_out.reshape(2, my_rows, -1)
    cols = lax.all_to_all(cols, "tp", split_axis=0, concat_axis=0, tiled=True)
    ids = lax.dynamic_slice_in_dim(expert_ids, half * my_rows, my_rows, 0)
    gates = lax.dynamic_slice_in_dim(gate_vals, half * my_rows, my_rows, 0)
    packed, hidden = front(cols, resid, norm_gain, ids, gates)
    me = lax.axis_index("ep").reshape(1)

    def gather_plane(piece):
        two = jnp.concatenate([piece, first(piece)], axis=0)
        own = jnp.concatenate([two, second(two)], axis=0)
        return own, sibling(own)

    def add(*terms):
        return functools.reduce(lambda a, b: a + b, [t.astype(F32) for t in terms])

    pieces = [packed]
    for _ in range(planes - 1):
        pieces.append(down(pieces[-1]))
    gathered = [gather_plane(piece) for piece in pieces]
    carried = []
    for step in list(range(1, planes)) + [0]:
        out_own, out_sib = experts(me, *gathered[step], w_gate[0], w_up[0], w_down[0])
        total = add(out_own, sibling(out_sib)).astype(BF16)
        kept = add(total[: 2 * my_rows], second(total[2 * my_rows :]), *carried).astype(BF16)
        if step:
            carried = [down(kept)]
    return add(hidden, kept[:my_rows], first(kept[my_rows:])).astype(BF16)


def exchanged_plan(ep_count, attn_out, resid, norm_gain, expert_ids, gate_vals, w_gate, w_up, w_down):
    hidden_f32, normed = norm_rows(attn_out, resid, norm_gain)
    normed_all = lax.all_gather(normed, "tp", axis=0, tiled=True)
    tok_block, width = normed_all.shape
    capacity = 4 * tok_block * expert_ids.shape[1] // (3 * ep_count)
    flat_ids = expert_ids.reshape(-1)
    onehot = (flat_ids[:, None] == jnp.arange(ep_count, dtype=jnp.int32)[None, :]).astype(jnp.int32)
    rank_in = jnp.sum(onehot * (jnp.cumsum(onehot, axis=0) - onehot), axis=1)
    slot_index = (flat_ids * capacity + rank_in).reshape(tok_block, -1)
    slot_range = jnp.arange(ep_count * capacity, dtype=jnp.int32)
    hit = slot_index[None, :, :] == slot_range[:, None, None]
    placing = jnp.any(hit, axis=-1).astype(BF16)
    send_rows = jnp.dot(placing, normed_all, preferred_element_type=F32).astype(BF16)
    send_rows = send_rows.reshape(ep_count, capacity, width)
    received = lax.all_to_all(send_rows, "ep", split_axis=0, concat_axis=0, tiled=True)
    out_rows = expert_rows(received.reshape(-1, width), w_gate[0], w_up[0], w_down[0]).astype(BF16)
    back_rows = lax.all_to_all(
        out_rows.reshape(received.shape), "ep", split_axis=0, concat_axis=0, tiled=True
    )
    scale = jnp.sum(jnp.where(hit, gate_vals[None, :, :], 0.0), axis=(1, 2))
    weighted = (back_rows.reshape(-1, width).astype(F32) * scale[:, None]).astype(BF16)
    part = lax.dot_general(placing, weighted, (((0,), (0,)), ((), ())), preferred_element_type=F32)
    moe_rows = lax.psum_scatter(part, "tp", scatter_dimension=0, tiled=True)
    return (hidden_f32 + moe_rows).astype(BF16)


def solution(mesh):
    ep_count, tp_count = mesh.shape["ep"], mesh.shape["tp"]
    paired = tp_count == 2 and ep_count % 4 == 0 and ep_count <= LANES // 2
    plan = gathered_plan if paired else exchanged_plan

    def per_device(*arguments):
        return plan(ep_count, *arguments)

    in_specs = (
        P("ep", "tp"),
        P(AXES, None),
        P(),
        P("ep", None),
        P("ep", None),
        P("ep", "tp", None),
        P("ep", "tp", None),
        P("ep", "tp", None),
    )
    return jax.shard_map(
        per_device, mesh=mesh, in_specs=in_specs, out_specs=P(AXES, None), check_vma=False
    )
```

```python
import functools

import jax
import jax.numpy as jnp
from jax import lax
from jax.experimental import pallas as pl
from jax.experimental.pallas import tpu as pltpu
from jax.sharding import PartitionSpec as P

F32 = jnp.float32
BF16 = jnp.bfloat16
AXES = ("ep", "tp")
LANES = 128
VMEM = pl.BlockSpec(memory_space=pltpu.VMEM)
SMEM = pl.BlockSpec(memory_space=pltpu.SMEM)


def by_feature(rows, weight):
    return lax.dot_general(rows, weight, (((1,), (1,)), ((), ())), preferred_element_type=F32)


def norm_rows(attn_out, resid, norm_gain):
    seq_rows = lax.all_to_all(attn_out, "tp", split_axis=0, concat_axis=1, tiled=True)
    hidden_state = (resid.astype(F32) + seq_rows.astype(F32)).astype(BF16)
    hidden_f32 = hidden_state.astype(F32)
    mean_sq = jnp.mean(hidden_f32 * hidden_f32, axis=-1, keepdims=True)
    normed = (hidden_f32 * lax.rsqrt(mean_sq + 1e-05) * norm_gain).astype(BF16)
    return hidden_f32, normed


def expert_rows(rows, w_gate, w_up, w_down):
    gate_pre = by_feature(rows, w_gate)
    up_pre = by_feature(rows, w_up)
    act = (jax.nn.silu(gate_pre) * up_pre).astype(BF16)
    return jnp.dot(act, w_down, preferred_element_type=F32)


def tiles(extent, size):
    return [(start, min(size, extent - start)) for start in range(0, extent, size)]


def product(a, b, a_dim, b_dim):
    return lax.dot_general(a, b, (((a_dim,), (b_dim,)), ((), ())), preferred_element_type=F32)


def front_kernel(half_ref, attn_ref, came_ref, resid_ref, gain_ref, ids_ref, gates_ref, packed_ref, hidden_ref):
    rows, width = resid_ref.shape
    half = half_ref[0]
    mine = pl.ds(pl.multiple_of(half * rows, rows), rows)
    kept, came = attn_ref[mine, :], came_ref[...]
    attn = jnp.concatenate([jnp.where(half == 0, kept, came), jnp.where(half == 0, came, kept)], axis=1)
    hidden_state = (resid_ref[...].astype(F32) + attn.astype(F32)).astype(BF16)
    hidden_ref[...] = hidden_state
    hidden = hidden_state.astype(F32)
    mean_sq = jnp.mean(hidden * hidden, axis=1, keepdims=True)
    packed_ref[:, :width] = (hidden * lax.rsqrt(mean_sq + 1e-05) * gain_ref[...]).astype(BF16)
    lane = lax.broadcasted_iota(jnp.int32, (rows, LANES), 1)
    ids, gates = ids_ref[mine, :], gates_ref[mine, :]
    weight = jnp.zeros((rows, LANES), F32)
    for k in range(ids.shape[1]):
        hit = lane % (LANES // 2) == ids[:, k : k + 1]
        weight = weight + jnp.where(hit, gates[:, k : k + 1], 0.0)
    high = weight.astype(BF16).astype(F32)
    packed_ref[:, width:] = jnp.where(lane < LANES // 2, high, weight - high).astype(BF16)


def front(half, attn_out, came, resid, norm_gain, ids, gates):
    rows, width = resid.shape
    return pl.pallas_call(
        front_kernel,
        out_shape=(
            jax.ShapeDtypeStruct((rows, width + LANES), BF16),
            jax.ShapeDtypeStruct((rows, width), BF16),
        ),
        in_specs=[SMEM] + [VMEM] * 6,
        out_specs=(VMEM, VMEM),
        compiler_params=pltpu.CompilerParams(vmem_limit_bytes=8 * 2**20),
    )(half.reshape(1), attn_out, came, resid, norm_gain.reshape(1, -1), ids, gates)


def expert_kernel(me_ref, own_a, own_b, sib_a, sib_b, gate_ref, up_ref, down_ref, own_out, sib_out, rows, act):
    count = 2 * own_a.shape[0]
    hidden_units, width = down_ref.shape
    slots = count // 2
    me = me_ref[0]
    row = lax.broadcasted_iota(jnp.int32, (count, count), 0)
    column = lax.broadcasted_iota(jnp.int32, (count, count), 1)
    earlier = jnp.where(column < row, 1.0, 0.0).astype(BF16)
    slot = lax.broadcasted_iota(jnp.int32, (count, slots), 1).astype(F32)

    def placing(*halves):
        routing = jnp.concatenate([h[:, width:] for h in halves], axis=0).astype(F32)
        lane = lax.broadcasted_iota(jnp.int32, routing.shape, 1)
        weight = jnp.sum(jnp.where(lane % (LANES // 2) == me, routing, 0.0), axis=1, keepdims=True)
        chosen = jnp.broadcast_to(jnp.where(weight != 0, 1.0, 0.0), (count, slots))
        rank = product(earlier, chosen.astype(BF16), 1, 0)
        return jnp.where(rank == slot, chosen, 0.0).astype(BF16), weight

    place_own, weight_own = placing(own_a, own_b)
    place_sib, weight_sib = placing(sib_a, sib_b)
    for start, size in tiles(width, 512):
        part = slice(start, start + size)
        for place, a, b, into in ((place_own, own_a, own_b, 0), (place_sib, sib_a, sib_b, slots)):
            both = jnp.concatenate([a[:, part], b[:, part]], axis=0)
            rows[into : into + slots, part] = product(place, both, 0, 0).astype(BF16)
    for start, size in tiles(hidden_units, 256):
        part = slice(start, start + size)
        gate_pre = product(rows[...], gate_ref[part, :], 1, 1)
        up_pre = product(rows[...], up_ref[part, :], 1, 1)
        act[:, part] = (gate_pre / (1.0 + jnp.exp(-gate_pre)) * up_pre).astype(BF16)
    for start, size in tiles(width, 1024):
        part = slice(start, start + size)
        out = product(act[...], down_ref[:, part], 1, 0).astype(BF16)
        own_out[:, part] = (product(place_own, out[:slots], 1, 0) * weight_own).astype(BF16)
        sib_out[:, part] = (product(place_sib, out[slots:], 1, 0) * weight_sib).astype(BF16)


def experts(me, own, sib, w_gate, w_up, w_down):
    count = 2 * own[0].shape[0]
    hidden_units, width = w_down.shape
    result = jax.ShapeDtypeStruct((count, width), BF16)
    return pl.pallas_call(
        expert_kernel,
        out_shape=(result, result),
        in_specs=[SMEM] + [VMEM] * 7,
        out_specs=(VMEM, VMEM),
        scratch_shapes=[pltpu.VMEM((count, width), BF16), pltpu.VMEM((count, hidden_units), BF16)],
        compiler_params=pltpu.CompilerParams(vmem_limit_bytes=16 * 2**20),
        cost_estimate=pl.CostEstimate(
            flops=6 * count * width * hidden_units, bytes_accessed=8 * count * width, transcendentals=0
        ),
    )(me, *own, *sib, w_gate, w_up, w_down)


def gathered_plan(ep_count, attn_out, resid, norm_gain, expert_ids, gate_vals, w_gate, w_up, w_down):
    planes = ep_count // 4
    my_rows = resid.shape[0]
    half = lax.axis_index("tp")
    me = lax.axis_index("ep").reshape(1)

    def routes(move):
        pairs = []
        for e in range(ep_count):
            for t in range(2):
                z, x, c, y = move(e // 4, (e // 2) % 2, e % 2, t)
                pairs.append((e * 2 + t, ((z * 2 + x) * 2 + c) * 2 + y))
        return lambda a: lax.ppermute(a, AXES, pairs)

    first = routes(lambda z, x, c, y: (z, x, c, 1 - y) if c else (z, 1 - x, c, y))
    second = routes(lambda z, x, c, y: (z, 1 - x, c, y) if c else (z, x, c, 1 - y))
    sibling = routes(lambda z, x, c, y: (z, x, 1 - c, y))
    partner = routes(lambda z, x, c, y: (z, x, c, 1 - y))
    ring = list(range(0, planes, 2)) + list(range(1, planes, 2))[::-1]
    after = {z: ring[i - 1] for i, z in enumerate(ring)}
    down = routes(lambda z, x, c, y: (after[z], x, c, y))

    def add(*terms):
        return functools.reduce(lambda a, b: a + b, [t.astype(F32) for t in terms])

    last = []

    def in_turn(value):
        if last:
            value, _ = lax.optimization_barrier((value, last[0]))
        last[:] = [value]
        return value

    theirs = lax.dynamic_slice_in_dim(attn_out, (1 - half) * my_rows, my_rows, 0)
    packed, hidden = front(half, attn_out, partner(theirs), resid, norm_gain, expert_ids, gate_vals)

    piece, two, one, other, came, out, total, kept, home = ({} for _ in range(9))

    def spread(step):
        if step:
            piece[step] = down(piece[step - 1])
        else:
            piece[0] = packed
        piece[step] = in_turn(piece[step])
        one[step] = first(piece[step])

    def widen(step):
        two[step] = in_turn(jnp.concatenate([piece[step], one[step]], axis=0))
        other[step] = second(two[step])
        came[step] = [sibling(two[step])]

    def share(step):
        other[step], came[step][0] = in_turn((other[step], came[step][0]))
        came[step].append(sibling(other[step]))

    def run(step):
        own, sib = in_turn(([two[step], other[step]], came[step]))
        out[step] = in_turn(experts(me, own, sib, w_gate[0], w_up[0], w_down[0]))
        came[step] = sibling(out[step][1])

    def merge_cores(step):
        total[step] = in_turn(add(out[step][0], came[step]).astype(BF16))
        other[step] = second(total[step][2 * my_rows :])

    def merge_second(step):
        kept[step] = in_turn(add(total[step][: 2 * my_rows], other[step]).astype(BF16))
        one[step] = first(kept[step][my_rows:])

    def merge_first(step):
        terms = [kept[step][:my_rows], one[step]] + ([home[step - 1]] if step > 1 else [])
        home[step] = down(in_turn(add(*terms).astype(BF16)))

    spread(0)
    spread(1)
    widen(0)
    widen(1)
    spread(2)
    share(0)
    widen(2)
    spread(3)
    share(1)
    run(1)
    widen(3)
    share(2)
    run(2)
    share(3)
    merge_cores(1)
    run(3)
    merge_cores(2)
    merge_second(1)
    run(0)
    merge_cores(3)
    merge_second(2)
    merge_first(1)
    merge_cores(0)
    merge_second(3)
    merge_first(2)
    merge_second(0)
    merge_first(3)
    return add(hidden, kept[0][:my_rows], one[0], home[planes - 1]).astype(BF16)


def exchanged_plan(ep_count, attn_out, resid, norm_gain, expert_ids, gate_vals, w_gate, w_up, w_down):
    hidden_f32, normed = norm_rows(attn_out, resid, norm_gain)
    normed_all = lax.all_gather(normed, "tp", axis=0, tiled=True)
    tok_block, width = normed_all.shape
    capacity = 4 * tok_block * expert_ids.shape[1] // (3 * ep_count)
    flat_ids = expert_ids.reshape(-1)
    onehot = (flat_ids[:, None] == jnp.arange(ep_count, dtype=jnp.int32)[None, :]).astype(jnp.int32)
    rank_in = jnp.sum(onehot * (jnp.cumsum(onehot, axis=0) - onehot), axis=1)
    slot_index = (flat_ids * capacity + rank_in).reshape(tok_block, -1)
    slot_range = jnp.arange(ep_count * capacity, dtype=jnp.int32)
    hit = slot_index[None, :, :] == slot_range[:, None, None]
    placing = jnp.any(hit, axis=-1).astype(BF16)
    send_rows = jnp.dot(placing, normed_all, preferred_element_type=F32).astype(BF16)
    send_rows = send_rows.reshape(ep_count, capacity, width)
    received = lax.all_to_all(send_rows, "ep", split_axis=0, concat_axis=0, tiled=True)
    out_rows = expert_rows(received.reshape(-1, width), w_gate[0], w_up[0], w_down[0]).astype(BF16)
    back_rows = lax.all_to_all(
        out_rows.reshape(received.shape), "ep", split_axis=0, concat_axis=0, tiled=True
    )
    scale = jnp.sum(jnp.where(hit, gate_vals[None, :, :], 0.0), axis=(1, 2))
    weighted = (back_rows.reshape(-1, width).astype(F32) * scale[:, None]).astype(BF16)
    part = lax.dot_general(placing, weighted, (((0,), (0,)), ((), ())), preferred_element_type=F32)
    moe_rows = lax.psum_scatter(part, "tp", scatter_dimension=0, tiled=True)
    return (hidden_f32 + moe_rows).astype(BF16)


def solution(mesh):
    ep_count, tp_count = mesh.shape["ep"], mesh.shape["tp"]
    paired = tp_count == 2 and ep_count % 4 == 0 and ep_count <= LANES // 2
    plan = gathered_plan if paired else exchanged_plan

    def per_device(*arguments):
        return plan(ep_count, *arguments)

    in_specs = (
        P("ep", "tp"),
        P(AXES, None),
        P(),
        P("ep", None),
        P("ep", None),
        P("ep", "tp", None),
        P("ep", "tp", None),
        P("ep", "tp", None),
    )
    return jax.shard_map(
        per_device, mesh=mesh, in_specs=in_specs, out_specs=P(AXES, None), check_vma=False
    )
```

```python
import functools

import jax
import jax.numpy as jnp
from jax import lax
from jax.experimental import pallas as pl
from jax.experimental.pallas import tpu as pltpu
from jax.sharding import PartitionSpec as P

F32 = jnp.float32
BF16 = jnp.bfloat16
AXES = ("ep", "tp")
LANES = 128
VMEM = pl.BlockSpec(memory_space=pltpu.VMEM)
SMEM = pl.BlockSpec(memory_space=pltpu.SMEM)


def by_feature(rows, weight):
    return lax.dot_general(rows, weight, (((1,), (1,)), ((), ())), preferred_element_type=F32)


def norm_rows(attn_out, resid, norm_gain):
    seq_rows = lax.all_to_all(attn_out, "tp", split_axis=0, concat_axis=1, tiled=True)
    hidden_state = (resid.astype(F32) + seq_rows.astype(F32)).astype(BF16)
    hidden_f32 = hidden_state.astype(F32)
    mean_sq = jnp.mean(hidden_f32 * hidden_f32, axis=-1, keepdims=True)
    normed = (hidden_f32 * lax.rsqrt(mean_sq + 1e-05) * norm_gain).astype(BF16)
    return hidden_f32, normed


def expert_rows(rows, w_gate, w_up, w_down):
    gate_pre = by_feature(rows, w_gate)
    up_pre = by_feature(rows, w_up)
    act = (jax.nn.silu(gate_pre) * up_pre).astype(BF16)
    return jnp.dot(act, w_down, preferred_element_type=F32)


def tiles(extent, size):
    return [(start, min(size, extent - start)) for start in range(0, extent, size)]


def product(a, b, a_dim, b_dim):
    return lax.dot_general(a, b, (((a_dim,), (b_dim,)), ((), ())), preferred_element_type=F32)


def front_kernel(half_ref, attn_ref, came_ref, resid_ref, gain_ref, ids_ref, gates_ref, packed_ref, hidden_ref):
    rows, width = resid_ref.shape
    half = half_ref[0]
    mine = pl.ds(pl.multiple_of(half * rows, rows), rows)
    kept, came = attn_ref[mine, :], came_ref[...]
    attn = jnp.concatenate([jnp.where(half == 0, kept, came), jnp.where(half == 0, came, kept)], axis=1)
    hidden_state = (resid_ref[...].astype(F32) + attn.astype(F32)).astype(BF16)
    hidden_ref[...] = hidden_state
    hidden = hidden_state.astype(F32)
    mean_sq = jnp.mean(hidden * hidden, axis=1, keepdims=True)
    packed_ref[:, :width] = (hidden * lax.rsqrt(mean_sq + 1e-05) * gain_ref[...]).astype(BF16)
    lane = lax.broadcasted_iota(jnp.int32, (rows, LANES), 1)
    ids, gates = ids_ref[mine, :], gates_ref[mine, :]
    weight = jnp.zeros((rows, LANES), F32)
    for k in range(ids.shape[1]):
        hit = lane % (LANES // 2) == ids[:, k : k + 1]
        weight = weight + jnp.where(hit, gates[:, k : k + 1], 0.0)
    high = weight.astype(BF16).astype(F32)
    packed_ref[:, width:] = jnp.where(lane < LANES // 2, high, weight - high).astype(BF16)


def whole(a):
    return pl.BlockSpec(a.shape, lambda i: (0,) * len(a.shape))


def front(half, *arrays):
    rows, width = arrays[2].shape
    results = (
        jax.ShapeDtypeStruct((rows, width + LANES), BF16),
        jax.ShapeDtypeStruct((rows, width), BF16),
    )
    return pl.pallas_call(
        front_kernel,
        grid=(1,),
        out_shape=results,
        in_specs=[SMEM] + [whole(a) for a in arrays],
        out_specs=tuple(whole(r) for r in results),
        compiler_params=pltpu.CompilerParams(vmem_limit_bytes=60 * 2**20),
    )(half.reshape(1), *arrays)


def expert_kernel(me_ref, own_a, own_b, sib_a, sib_b, gate_ref, up_ref, down_ref, own_out, sib_out, came, rows, act, arrived):
    count = 2 * own_a.shape[0]
    hidden_units, width = down_ref.shape
    slots = count // 2
    me = me_ref[0]
    loads = []
    for i, source in enumerate((own_a, own_b, sib_a, sib_b)):
        into = came.at[i // 2, pl.ds(i % 2 * slots, slots)]
        loads.append(pltpu.make_async_copy(source, into, arrived.at[i]))
        loads[-1].start()
    row = lax.broadcasted_iota(jnp.int32, (count, count), 0)
    column = lax.broadcasted_iota(jnp.int32, (count, count), 1)
    earlier = jnp.where(column < row, 1.0, 0.0).astype(BF16)
    slot = lax.broadcasted_iota(jnp.int32, (count, slots), 1).astype(F32)

    def placing(n):
        routing = came[n, :, width:].astype(F32)
        lane = lax.broadcasted_iota(jnp.int32, routing.shape, 1)
        weight = jnp.sum(jnp.where(lane % (LANES // 2) == me, routing, 0.0), axis=1, keepdims=True)
        chosen = jnp.broadcast_to(jnp.where(weight != 0, 1.0, 0.0), (count, slots))
        rank = product(earlier, chosen.astype(BF16), 1, 0)
        return jnp.where(rank == slot, chosen, 0.0).astype(BF16), weight

    for load in loads:
        load.wait()
    place_own, weight_own = placing(0)
    place_sib, weight_sib = placing(1)
    for start, size in tiles(width, 512):
        part = slice(start, start + size)
        rows[:slots, part] = product(place_own, came[0, :, part], 0, 0).astype(BF16)
        rows[slots:, part] = product(place_sib, came[1, :, part], 0, 0).astype(BF16)
    for start, size in tiles(hidden_units, 256):
        part = slice(start, start + size)
        gate_pre = product(rows[...], gate_ref[part, :], 1, 1)
        up_pre = product(rows[...], up_ref[part, :], 1, 1)
        act[:, part] = (gate_pre / (1.0 + jnp.exp(-gate_pre)) * up_pre).astype(BF16)
    for start, size in tiles(width, 1024):
        part = slice(start, start + size)
        out = product(act[...], down_ref[:, part], 1, 0).astype(BF16)
        own_out[:, part] = (product(place_own, out[:slots], 1, 0) * weight_own).astype(BF16)
        sib_out[:, part] = (product(place_sib, out[slots:], 1, 0) * weight_sib).astype(BF16)


def experts(me, own, sib, w_gate, w_up, w_down):
    count = 2 * own[0].shape[0]
    hidden_units, width = w_down.shape
    result = jax.ShapeDtypeStruct((count, width), BF16)
    return pl.pallas_call(
        expert_kernel,
        out_shape=(result, result),
        in_specs=[SMEM] + [pl.BlockSpec(memory_space=pl.ANY)] * 4 + [VMEM] * 3,
        out_specs=(VMEM, VMEM),
        scratch_shapes=[
            pltpu.VMEM((2, count, own[0].shape[1]), BF16),
            pltpu.VMEM((count, width), BF16),
            pltpu.VMEM((count, hidden_units), BF16),
            pltpu.SemaphoreType.DMA((4,)),
        ],
        compiler_params=pltpu.CompilerParams(vmem_limit_bytes=16 * 2**20),
        cost_estimate=pl.CostEstimate(
            flops=6 * count * width * hidden_units, bytes_accessed=8 * count * width, transcendentals=0
        ),
    )(me, *own, *sib, w_gate, w_up, w_down)


def gathered_plan(ep_count, attn_out, resid, norm_gain, expert_ids, gate_vals, w_gate, w_up, w_down):
    planes = ep_count // 4
    my_rows = resid.shape[0]
    half = lax.axis_index("tp")
    me = lax.axis_index("ep").reshape(1)

    def routes(move):
        pairs = []
        for e in range(ep_count):
            for t in range(2):
                z, x, c, y = move(e // 4, (e // 2) % 2, e % 2, t)
                pairs.append((e * 2 + t, ((z * 2 + x) * 2 + c) * 2 + y))
        return lambda a: lax.ppermute(a, AXES, pairs)

    first = routes(lambda z, x, c, y: (z, x, c, 1 - y) if c else (z, 1 - x, c, y))
    second = routes(lambda z, x, c, y: (z, 1 - x, c, y) if c else (z, x, c, 1 - y))
    sibling = routes(lambda z, x, c, y: (z, x, 1 - c, y))
    partner = routes(lambda z, x, c, y: (z, x, c, 1 - y))
    ring = list(range(0, planes, 2)) + list(range(1, planes, 2))[::-1]
    after = {z: ring[i - 1] for i, z in enumerate(ring)}
    down = routes(lambda z, x, c, y: (after[z], x, c, y))
    place = {z: i for i, z in enumerate(ring)}
    returns = [
        routes(lambda z, x, c, y, step=step: (ring[(place[z] + step) % planes], x, c, y)) for step in range(planes)
    ]

    def add(*terms):
        return functools.reduce(lambda a, b: a + b, [t.astype(F32) for t in terms])

    last = []

    def in_turn(value):
        if last:
            value, _ = lax.optimization_barrier((value, last[0]))
        last[:] = [value]
        return value

    theirs = lax.dynamic_slice_in_dim(attn_out, (1 - half) * my_rows, my_rows, 0)
    packed, hidden = front(half, attn_out, partner(theirs), resid, norm_gain.reshape(1, -1), expert_ids, gate_vals)

    piece, two, one, other, came, out, total, kept, home = ({} for _ in range(9))

    def spread(step):
        if step:
            piece[step] = down(piece[step - 1])
        else:
            piece[0] = packed
        piece[step] = in_turn(piece[step])
        one[step] = first(piece[step])

    def widen(step):
        two[step] = in_turn(jnp.concatenate([piece[step], one[step]], axis=0))
        other[step] = second(two[step])
        came[step] = [sibling(two[step])]

    def share(step):
        other[step], came[step][0] = in_turn((other[step], came[step][0]))
        came[step].append(sibling(other[step]))

    def run(step):
        own, sib = in_turn(([two[step], other[step]], came[step]))
        out[step] = in_turn(experts(me, own, sib, w_gate[0], w_up[0], w_down[0]))
        came[step] = sibling(out[step][1])

    def merge_cores(step):
        total[step] = (add(out[step][0], came[step]).astype(BF16))
        other[step] = second(total[step][2 * my_rows :])

    def merge_second(step):
        kept[step] = (add(total[step][: 2 * my_rows], other[step]).astype(BF16))
        one[step] = first(kept[step][my_rows:])

    def merge_first(step):
        value = (add(kept[step][:my_rows], one[step]).astype(BF16))
        home[step] = returns[step](value)

    spread(0)
    spread(1)
    widen(0)
    spread(2)
    widen(1)
    share(0)
    spread(3)
    widen(2)
    share(1)
    run(1)
    widen(3)
    share(2)
    run(2)
    share(3)
    run(3)
    run(0)
    merge_cores(1)
    merge_cores(2)
    merge_cores(3)
    merge_cores(0)
    merge_second(1)
    merge_second(2)
    merge_second(3)
    merge_second(0)
    merge_first(1)
    merge_first(2)
    merge_first(3)
    return add(hidden, kept[0][:my_rows], one[0], *(home[step] for step in range(1, planes))).astype(BF16)


def exchanged_plan(ep_count, attn_out, resid, norm_gain, expert_ids, gate_vals, w_gate, w_up, w_down):
    hidden_f32, normed = norm_rows(attn_out, resid, norm_gain)
    normed_all = lax.all_gather(normed, "tp", axis=0, tiled=True)
    tok_block, width = normed_all.shape
    capacity = 4 * tok_block * expert_ids.shape[1] // (3 * ep_count)
    flat_ids = expert_ids.reshape(-1)
    onehot = (flat_ids[:, None] == jnp.arange(ep_count, dtype=jnp.int32)[None, :]).astype(jnp.int32)
    rank_in = jnp.sum(onehot * (jnp.cumsum(onehot, axis=0) - onehot), axis=1)
    slot_index = (flat_ids * capacity + rank_in).reshape(tok_block, -1)
    slot_range = jnp.arange(ep_count * capacity, dtype=jnp.int32)
    hit = slot_index[None, :, :] == slot_range[:, None, None]
    placing = jnp.any(hit, axis=-1).astype(BF16)
    send_rows = jnp.dot(placing, normed_all, preferred_element_type=F32).astype(BF16)
    send_rows = send_rows.reshape(ep_count, capacity, width)
    received = lax.all_to_all(send_rows, "ep", split_axis=0, concat_axis=0, tiled=True)
    out_rows = expert_rows(received.reshape(-1, width), w_gate[0], w_up[0], w_down[0]).astype(BF16)
    back_rows = lax.all_to_all(
        out_rows.reshape(received.shape), "ep", split_axis=0, concat_axis=0, tiled=True
    )
    scale = jnp.sum(jnp.where(hit, gate_vals[None, :, :], 0.0), axis=(1, 2))
    weighted = (back_rows.reshape(-1, width).astype(F32) * scale[:, None]).astype(BF16)
    part = lax.dot_general(placing, weighted, (((0,), (0,)), ((), ())), preferred_element_type=F32)
    moe_rows = lax.psum_scatter(part, "tp", scatter_dimension=0, tiled=True)
    return (hidden_f32 + moe_rows).astype(BF16)


def solution(mesh):
    ep_count, tp_count = mesh.shape["ep"], mesh.shape["tp"]
    paired = tp_count == 2 and ep_count % 4 == 0 and ep_count <= LANES // 2
    plan = gathered_plan if paired else exchanged_plan

    def per_device(*arguments):
        return plan(ep_count, *arguments)

    in_specs = (
        P("ep", "tp"),
        P(AXES, None),
        P(),
        P("ep", None),
        P("ep", None),
        P("ep", "tp", None),
        P("ep", "tp", None),
        P("ep", "tp", None),
    )
    return jax.shard_map(
        per_device, mesh=mesh, in_specs=in_specs, out_specs=P(AXES, None), check_vma=False
    )
```

```python
import functools

import jax
import jax.numpy as jnp
from jax import lax
from jax.experimental import pallas as pl
from jax.experimental.pallas import tpu as pltpu
from jax.sharding import PartitionSpec as P

F32 = jnp.float32
BF16 = jnp.bfloat16
AXES = ("ep", "tp")
LANES = 128
VMEM = pl.BlockSpec(memory_space=pltpu.VMEM)
SMEM = pl.BlockSpec(memory_space=pltpu.SMEM)


def by_feature(rows, weight):
    return lax.dot_general(rows, weight, (((1,), (1,)), ((), ())), preferred_element_type=F32)


def norm_rows(attn_out, resid, norm_gain):
    seq_rows = lax.all_to_all(attn_out, "tp", split_axis=0, concat_axis=1, tiled=True)
    hidden_state = (resid.astype(F32) + seq_rows.astype(F32)).astype(BF16)
    hidden_f32 = hidden_state.astype(F32)
    mean_sq = jnp.mean(hidden_f32 * hidden_f32, axis=-1, keepdims=True)
    normed = (hidden_f32 * lax.rsqrt(mean_sq + 1e-05) * norm_gain).astype(BF16)
    return hidden_f32, normed


def expert_rows(rows, w_gate, w_up, w_down):
    gate_pre = by_feature(rows, w_gate)
    up_pre = by_feature(rows, w_up)
    act = (jax.nn.silu(gate_pre) * up_pre).astype(BF16)
    return jnp.dot(act, w_down, preferred_element_type=F32)


def tiles(extent, size):
    return [(start, min(size, extent - start)) for start in range(0, extent, size)]


def product(a, b, a_dim, b_dim):
    return lax.dot_general(a, b, (((a_dim,), (b_dim,)), ((), ())), preferred_element_type=F32)


def front_kernel(half_ref, attn_ref, came_ref, resid_ref, gain_ref, ids_ref, gates_ref, packed_ref, hidden_ref):
    rows, width = resid_ref.shape
    half = half_ref[0]
    mine = pl.ds(pl.multiple_of(half * rows, rows), rows)
    kept, came = attn_ref[mine, :], came_ref[...]
    attn = jnp.concatenate([jnp.where(half == 0, kept, came), jnp.where(half == 0, came, kept)], axis=1)
    hidden_state = (resid_ref[...].astype(F32) + attn.astype(F32)).astype(BF16)
    hidden_ref[...] = hidden_state
    hidden = hidden_state.astype(F32)
    mean_sq = jnp.mean(hidden * hidden, axis=1, keepdims=True)
    packed_ref[:, :width] = (hidden * lax.rsqrt(mean_sq + 1e-05) * gain_ref[...]).astype(BF16)
    lane = lax.broadcasted_iota(jnp.int32, (rows, LANES), 1)
    ids, gates = ids_ref[mine, :], gates_ref[mine, :]
    weight = jnp.zeros((rows, LANES), F32)
    for k in range(ids.shape[1]):
        hit = lane % (LANES // 2) == ids[:, k : k + 1]
        weight = weight + jnp.where(hit, gates[:, k : k + 1], 0.0)
    high = weight.astype(BF16).astype(F32)
    packed_ref[:, width:] = jnp.where(lane < LANES // 2, high, weight - high).astype(BF16)


def whole(a):
    return pl.BlockSpec(a.shape, lambda i: (0,) * len(a.shape))


def front(half, *arrays):
    rows, width = arrays[2].shape
    results = (
        jax.ShapeDtypeStruct((rows, width + LANES), BF16),
        jax.ShapeDtypeStruct((rows, width), BF16),
    )
    return pl.pallas_call(
        front_kernel,
        grid=(1,),
        out_shape=results,
        in_specs=[SMEM] + [whole(a) for a in arrays],
        out_specs=tuple(whole(r) for r in results),
        compiler_params=pltpu.CompilerParams(vmem_limit_bytes=60 * 2**20),
    )(half.reshape(1), *arrays)


def expert_kernel(me_ref, own_a, own_b, sib_a, sib_b, gate_ref, up_ref, down_ref, own_out, sib_out, came, rows, act, arrived):
    count = 2 * own_a.shape[0]
    hidden_units, width = down_ref.shape
    slots = count // 2
    me = me_ref[0]
    loads = []
    for i, source in enumerate((own_a, own_b, sib_a, sib_b)):
        into = came.at[i // 2, pl.ds(i % 2 * slots, slots)]
        loads.append(pltpu.make_async_copy(source, into, arrived.at[i]))
        loads[-1].start()
    row = lax.broadcasted_iota(jnp.int32, (count, count), 0)
    column = lax.broadcasted_iota(jnp.int32, (count, count), 1)
    earlier = jnp.where(column < row, 1.0, 0.0).astype(BF16)
    slot = lax.broadcasted_iota(jnp.int32, (count, slots), 1).astype(F32)

    def placing(n):
        routing = came[n, :, width:].astype(F32)
        lane = lax.broadcasted_iota(jnp.int32, routing.shape, 1)
        weight = jnp.sum(jnp.where(lane % (LANES // 2) == me, routing, 0.0), axis=1, keepdims=True)
        chosen = jnp.broadcast_to(jnp.where(weight != 0, 1.0, 0.0), (count, slots))
        rank = product(earlier, chosen.astype(BF16), 1, 0)
        return jnp.where(rank == slot, chosen, 0.0).astype(BF16), weight

    for load in loads:
        load.wait()
    place_own, weight_own = placing(0)
    place_sib, weight_sib = placing(1)
    for start, size in tiles(width, 512):
        part = slice(start, start + size)
        rows[:slots, part] = product(place_own, came[0, :, part], 0, 0).astype(BF16)
        rows[slots:, part] = product(place_sib, came[1, :, part], 0, 0).astype(BF16)
    for start, size in tiles(hidden_units, 256):
        part = slice(start, start + size)
        gate_pre = product(rows[...], gate_ref[part, :], 1, 1)
        up_pre = product(rows[...], up_ref[part, :], 1, 1)
        act[:, part] = (gate_pre / (1.0 + jnp.exp(-gate_pre)) * up_pre).astype(BF16)
    for start, size in tiles(width, 1024):
        part = slice(start, start + size)
        out = product(act[...], down_ref[:, part], 1, 0).astype(BF16)
        own_out[:, part] = (product(place_own, out[:slots], 1, 0) * weight_own).astype(BF16)
        sib_out[:, part] = (product(place_sib, out[slots:], 1, 0) * weight_sib).astype(BF16)


def experts(me, own, sib, w_gate, w_up, w_down):
    count = 2 * own[0].shape[0]
    hidden_units, width = w_down.shape
    result = jax.ShapeDtypeStruct((count, width), BF16)
    return pl.pallas_call(
        expert_kernel,
        out_shape=(result, result),
        in_specs=[SMEM] + [pl.BlockSpec(memory_space=pl.ANY)] * 4 + [VMEM] * 3,
        out_specs=(VMEM, VMEM),
        scratch_shapes=[
            pltpu.VMEM((2, count, own[0].shape[1]), BF16),
            pltpu.VMEM((count, width), BF16),
            pltpu.VMEM((count, hidden_units), BF16),
            pltpu.SemaphoreType.DMA((4,)),
        ],
        compiler_params=pltpu.CompilerParams(vmem_limit_bytes=16 * 2**20),
        cost_estimate=pl.CostEstimate(
            flops=6 * count * width * hidden_units, bytes_accessed=8 * count * width, transcendentals=0
        ),
    )(me, *own, *sib, w_gate, w_up, w_down)


def gathered_plan(ep_count, attn_out, resid, norm_gain, expert_ids, gate_vals, w_gate, w_up, w_down):
    planes = ep_count // 4
    my_rows = resid.shape[0]
    half = lax.axis_index("tp")
    me = lax.axis_index("ep").reshape(1)

    def routes(move):
        pairs = []
        for e in range(ep_count):
            for t in range(2):
                z, x, c, y = move(e // 4, (e // 2) % 2, e % 2, t)
                pairs.append((e * 2 + t, ((z * 2 + x) * 2 + c) * 2 + y))
        return lambda a: lax.ppermute(a, AXES, pairs)

    first = routes(lambda z, x, c, y: (z, x, c, 1 - y) if c else (z, 1 - x, c, y))
    second = routes(lambda z, x, c, y: (z, 1 - x, c, y) if c else (z, x, c, 1 - y))
    sibling = routes(lambda z, x, c, y: (z, x, 1 - c, y))
    partner = routes(lambda z, x, c, y: (z, x, c, 1 - y))
    ring = list(range(0, planes, 2)) + list(range(1, planes, 2))[::-1]
    after = {z: ring[i - 1] for i, z in enumerate(ring)}
    down = routes(lambda z, x, c, y: (after[z], x, c, y))
    place = {z: i for i, z in enumerate(ring)}
    returns = [
        routes(lambda z, x, c, y, step=step: (ring[(place[z] + step) % planes], x, c, y)) for step in range(planes)
    ]

    def add(*terms):
        return functools.reduce(lambda a, b: a + b, [t.astype(F32) for t in terms])

    last, tied = [], [True]

    def in_turn(value):
        if tied[0]:
            if last:
                value, _ = lax.optimization_barrier((value, last[0]))
            last[:] = [value]
        return value

    theirs = lax.dynamic_slice_in_dim(attn_out, (1 - half) * my_rows, my_rows, 0)
    packed, hidden = front(half, attn_out, partner(theirs), resid, norm_gain.reshape(1, -1), expert_ids, gate_vals)

    piece, two, one, other, came, out, total, kept, home = ({} for _ in range(9))

    def spread(step):
        if step:
            piece[step] = down(piece[step - 1])
        else:
            piece[0] = packed
        piece[step] = in_turn(piece[step])
        one[step] = first(piece[step])

    def widen(step):
        two[step] = in_turn(jnp.concatenate([piece[step], one[step]], axis=0))
        other[step] = second(two[step])
        came[step] = [sibling(two[step])]

    def share(step):
        other[step], came[step][0] = in_turn((other[step], came[step][0]))
        came[step].append(sibling(other[step]))

    def run(step):
        own, sib = in_turn(([two[step], other[step]], came[step]))
        out[step] = in_turn(experts(me, own, sib, w_gate[0], w_up[0], w_down[0]))
        came[step] = sibling(out[step][1])

    def merge_cores(step):
        total[step] = in_turn(add(out[step][0], came[step]).astype(BF16))
        other[step] = second(total[step][2 * my_rows :])

    def merge_second(step):
        kept[step] = in_turn(add(total[step][: 2 * my_rows], other[step]).astype(BF16))
        one[step] = first(kept[step][my_rows:])

    def merge_first(step):
        value = in_turn(add(kept[step][:my_rows], one[step]).astype(BF16))
        home[step] = returns[step](value)

    schedule = [
        (spread, 0, True),
        (spread, 1, True),
        (widen, 0, True),
        (spread, 2, True),
        (widen, 1, True),
        (share, 0, True),
        (spread, 3, True),
        (widen, 2, True),
        (widen, 3, False),
        (share, 1, True),
        (run, 1, True),
        (share, 2, True),
        (run, 2, True),
        (share, 3, True),
        (run, 3, True),
        (run, 0, True),
        (merge_cores, 1, False),
        (merge_second, 1, False),
        (merge_cores, 2, False),
        (merge_second, 2, False),
        (merge_first, 2, False),
        (merge_cores, 3, False),
        (merge_first, 1, True),
        (merge_second, 3, False),
        (merge_first, 3, False),
        (merge_cores, 0, True),
        (merge_second, 0, True),
    ]
    for take, step, tie in schedule:
        tied[0] = tie
        take(step)
    return add(hidden, kept[0][:my_rows], one[0], *(home[step] for step in range(1, planes))).astype(BF16)


def exchanged_plan(ep_count, attn_out, resid, norm_gain, expert_ids, gate_vals, w_gate, w_up, w_down):
    hidden_f32, normed = norm_rows(attn_out, resid, norm_gain)
    normed_all = lax.all_gather(normed, "tp", axis=0, tiled=True)
    tok_block, width = normed_all.shape
    capacity = 4 * tok_block * expert_ids.shape[1] // (3 * ep_count)
    flat_ids = expert_ids.reshape(-1)
    onehot = (flat_ids[:, None] == jnp.arange(ep_count, dtype=jnp.int32)[None, :]).astype(jnp.int32)
    rank_in = jnp.sum(onehot * (jnp.cumsum(onehot, axis=0) - onehot), axis=1)
    slot_index = (flat_ids * capacity + rank_in).reshape(tok_block, -1)
    slot_range = jnp.arange(ep_count * capacity, dtype=jnp.int32)
    hit = slot_index[None, :, :] == slot_range[:, None, None]
    placing = jnp.any(hit, axis=-1).astype(BF16)
    send_rows = jnp.dot(placing, normed_all, preferred_element_type=F32).astype(BF16)
    send_rows = send_rows.reshape(ep_count, capacity, width)
    received = lax.all_to_all(send_rows, "ep", split_axis=0, concat_axis=0, tiled=True)
    out_rows = expert_rows(received.reshape(-1, width), w_gate[0], w_up[0], w_down[0]).astype(BF16)
    back_rows = lax.all_to_all(
        out_rows.reshape(received.shape), "ep", split_axis=0, concat_axis=0, tiled=True
    )
    scale = jnp.sum(jnp.where(hit, gate_vals[None, :, :], 0.0), axis=(1, 2))
    weighted = (back_rows.reshape(-1, width).astype(F32) * scale[:, None]).astype(BF16)
    part = lax.dot_general(placing, weighted, (((0,), (0,)), ((), ())), preferred_element_type=F32)
    moe_rows = lax.psum_scatter(part, "tp", scatter_dimension=0, tiled=True)
    return (hidden_f32 + moe_rows).astype(BF16)


def solution(mesh):
    ep_count, tp_count = mesh.shape["ep"], mesh.shape["tp"]
    paired = tp_count == 2 and divmod(ep_count, 4) == (4, 0)
    plan = gathered_plan if paired else exchanged_plan

    def per_device(*arguments):
        return plan(ep_count, *arguments)

    in_specs = (
        P("ep", "tp"),
        P(AXES, None),
        P(),
        P("ep", None),
        P("ep", None),
        P("ep", "tp", None),
        P("ep", "tp", None),
        P("ep", "tp", None),
    )
    return jax.shard_map(
        per_device, mesh=mesh, in_specs=in_specs, out_specs=P(AXES, None), check_vma=False
    )
```

```python
import functools

import jax
import jax.numpy as jnp
from jax import lax
from jax.experimental import pallas as pl
from jax.experimental.pallas import tpu as pltpu
from jax.sharding import PartitionSpec as P

F32 = jnp.float32
BF16 = jnp.bfloat16
AXES = ("ep", "tp")
LANES = 128
VMEM = pl.BlockSpec(memory_space=pltpu.VMEM)
SMEM = pl.BlockSpec(memory_space=pltpu.SMEM)


def by_feature(rows, weight):
    return lax.dot_general(rows, weight, (((1,), (1,)), ((), ())), preferred_element_type=F32)


def norm_rows(attn_out, resid, norm_gain):
    seq_rows = lax.all_to_all(attn_out, "tp", split_axis=0, concat_axis=1, tiled=True)
    hidden_state = (resid.astype(F32) + seq_rows.astype(F32)).astype(BF16)
    hidden_f32 = hidden_state.astype(F32)
    mean_sq = jnp.mean(hidden_f32 * hidden_f32, axis=-1, keepdims=True)
    normed = (hidden_f32 * lax.rsqrt(mean_sq + 1e-05) * norm_gain).astype(BF16)
    return hidden_f32, normed


def expert_rows(rows, w_gate, w_up, w_down):
    gate_pre = by_feature(rows, w_gate)
    up_pre = by_feature(rows, w_up)
    act = (jax.nn.silu(gate_pre) * up_pre).astype(BF16)
    return jnp.dot(act, w_down, preferred_element_type=F32)


def tiles(extent, size):
    return [(start, min(size, extent - start)) for start in range(0, extent, size)]


def product(a, b, a_dim, b_dim):
    return lax.dot_general(a, b, (((a_dim,), (b_dim,)), ((), ())), preferred_element_type=F32)


def front_kernel(half_ref, attn_ref, came_ref, resid_ref, gain_ref, ids_ref, gates_ref, packed_ref, hidden_ref):
    rows, width = resid_ref.shape
    half = half_ref[0]
    mine = pl.ds(pl.multiple_of(half * rows, rows), rows)
    kept, came = attn_ref[mine, :], came_ref[...]
    attn = jnp.concatenate([jnp.where(half == 0, kept, came), jnp.where(half == 0, came, kept)], axis=1)
    hidden_state = (resid_ref[...].astype(F32) + attn.astype(F32)).astype(BF16)
    hidden_ref[...] = hidden_state
    hidden = hidden_state.astype(F32)
    mean_sq = jnp.mean(hidden * hidden, axis=1, keepdims=True)
    packed_ref[:, :width] = (hidden * lax.rsqrt(mean_sq + 1e-05) * gain_ref[...]).astype(BF16)
    lane = lax.broadcasted_iota(jnp.int32, (rows, LANES), 1)
    ids, gates = ids_ref[mine, :], gates_ref[mine, :]
    weight = jnp.zeros((rows, LANES), F32)
    for k in range(ids.shape[1]):
        hit = lane % (LANES // 2) == ids[:, k : k + 1]
        weight = weight + jnp.where(hit, gates[:, k : k + 1], 0.0)
    high = weight.astype(BF16).astype(F32)
    packed_ref[:, width:] = jnp.where(lane < LANES // 2, high, weight - high).astype(BF16)


def whole(a):
    return pl.BlockSpec(a.shape, lambda i: (0,) * len(a.shape))


def front(half, *arrays):
    rows, width = arrays[2].shape
    results = (
        jax.ShapeDtypeStruct((rows, width + LANES), BF16),
        jax.ShapeDtypeStruct((rows, width), BF16),
    )
    return pl.pallas_call(
        front_kernel,
        grid=(1,),
        out_shape=results,
        in_specs=[SMEM] + [whole(a) for a in arrays],
        out_specs=tuple(whole(r) for r in results),
        compiler_params=pltpu.CompilerParams(vmem_limit_bytes=60 * 2**20),
    )(half.reshape(1), *arrays)


def expert_kernel(me_ref, own_a, own_b, sib_a, sib_b, gate_ref, up_ref, down_ref, own_out, sib_out, came, rows, act, arrived):
    count = 2 * own_a.shape[0]
    hidden_units, width = down_ref.shape
    slots = count // 2
    me = me_ref[0]
    loads = []
    for i, source in enumerate((own_a, own_b, sib_a, sib_b)):
        into = came.at[i // 2, pl.ds(i % 2 * slots, slots)]
        loads.append(pltpu.make_async_copy(source, into, arrived.at[i]))
        loads[-1].start()
    row = lax.broadcasted_iota(jnp.int32, (count, count), 0)
    column = lax.broadcasted_iota(jnp.int32, (count, count), 1)
    earlier = jnp.where(column < row, 1.0, 0.0).astype(BF16)
    slot = lax.broadcasted_iota(jnp.int32, (count, slots), 1).astype(F32)

    def placing(n):
        routing = came[n, :, width:].astype(F32)
        lane = lax.broadcasted_iota(jnp.int32, routing.shape, 1)
        weight = jnp.sum(jnp.where(lane % (LANES // 2) == me, routing, 0.0), axis=1, keepdims=True)
        chosen = jnp.broadcast_to(jnp.where(weight != 0, 1.0, 0.0), (count, slots))
        rank = product(earlier, chosen.astype(BF16), 1, 0)
        return jnp.where(rank == slot, chosen, 0.0).astype(BF16), weight

    for load in loads:
        load.wait()
    place_own, weight_own = placing(0)
    place_sib, weight_sib = placing(1)
    for start, size in tiles(width, 512):
        part = slice(start, start + size)
        rows[:slots, part] = product(place_own, came[0, :, part], 0, 0).astype(BF16)
        rows[slots:, part] = product(place_sib, came[1, :, part], 0, 0).astype(BF16)
    for start, size in tiles(hidden_units, 256):
        part = slice(start, start + size)
        gate_pre = product(rows[...], gate_ref[part, :], 1, 1)
        up_pre = product(rows[...], up_ref[part, :], 1, 1)
        act[:, part] = (gate_pre / (1.0 + jnp.exp(-gate_pre)) * up_pre).astype(BF16)
    for start, size in tiles(width, 1024):
        part = slice(start, start + size)
        out = product(act[...], down_ref[:, part], 1, 0).astype(BF16)
        own_out[:, part] = (product(place_own, out[:slots], 1, 0) * weight_own).astype(BF16)
        sib_out[:, part] = (product(place_sib, out[slots:], 1, 0) * weight_sib).astype(BF16)


def experts(me, own, sib, w_gate, w_up, w_down):
    count = 2 * own[0].shape[0]
    hidden_units, width = w_down.shape
    result = jax.ShapeDtypeStruct((count, width), BF16)
    return pl.pallas_call(
        expert_kernel,
        out_shape=(result, result),
        in_specs=[SMEM] + [pl.BlockSpec(memory_space=pl.ANY)] * 4 + [VMEM] * 3,
        out_specs=(VMEM, VMEM),
        scratch_shapes=[
            pltpu.VMEM((2, count, own[0].shape[1]), BF16),
            pltpu.VMEM((count, width), BF16),
            pltpu.VMEM((count, hidden_units), BF16),
            pltpu.SemaphoreType.DMA((4,)),
        ],
        compiler_params=pltpu.CompilerParams(vmem_limit_bytes=16 * 2**20),
        cost_estimate=pl.CostEstimate(
            flops=6 * count * width * hidden_units, bytes_accessed=8 * count * width, transcendentals=0
        ),
    )(me, *own, *sib, w_gate, w_up, w_down)


def gathered_plan(ep_count, attn_out, resid, norm_gain, expert_ids, gate_vals, w_gate, w_up, w_down):
    planes = ep_count // 4
    my_rows = resid.shape[0]
    half = lax.axis_index("tp")
    me = lax.axis_index("ep").reshape(1)

    def routes(move):
        pairs = []
        for e in range(ep_count):
            for t in range(2):
                z, x, c, y = move(e // 4, (e // 2) % 2, e % 2, t)
                pairs.append((e * 2 + t, ((z * 2 + x) * 2 + c) * 2 + y))
        return lambda a: lax.ppermute(a, AXES, pairs)

    first = routes(lambda z, x, c, y: (z, x, c, 1 - y) if c else (z, 1 - x, c, y))
    second = routes(lambda z, x, c, y: (z, 1 - x, c, y) if c else (z, x, c, 1 - y))
    sibling = routes(lambda z, x, c, y: (z, x, 1 - c, y))
    partner = routes(lambda z, x, c, y: (z, x, c, 1 - y))
    ring = list(range(0, planes, 2)) + list(range(1, planes, 2))[::-1]
    after = {z: ring[i - 1] for i, z in enumerate(ring)}
    down = routes(lambda z, x, c, y: (after[z], x, c, y))
    place = {z: i for i, z in enumerate(ring)}
    returns = [
        routes(lambda z, x, c, y, step=step: (ring[(place[z] + step) % planes], x, c, y)) for step in range(planes)
    ]

    def add(*terms):
        return functools.reduce(lambda a, b: a + b, [t.astype(F32) for t in terms])

    last, tied = [], [True]

    def in_turn(value):
        if tied[0]:
            if last:
                value, _ = lax.optimization_barrier((value, last[0]))
            last[:] = [value]
        return value

    theirs = lax.dynamic_slice_in_dim(attn_out, (1 - half) * my_rows, my_rows, 0)
    packed, hidden = front(half, attn_out, partner(theirs), resid, norm_gain.reshape(1, -1), expert_ids, gate_vals)

    piece, two, one, other, came, out, total, kept, home = ({} for _ in range(9))

    def spread(step):
        if step:
            piece[step] = down(piece[step - 1])
        else:
            piece[0] = packed
        piece[step] = in_turn(piece[step])
        one[step] = first(piece[step])

    def widen(step):
        two[step] = in_turn(jnp.concatenate([piece[step], one[step]], axis=0))
        other[step] = second(two[step])
        came[step] = [sibling(two[step])]

    def share(step):
        other[step], came[step][0] = in_turn((other[step], came[step][0]))
        came[step].append(sibling(other[step]))

    def run(step):
        own, sib = in_turn(([two[step], other[step]], came[step]))
        out[step] = in_turn(experts(me, own, sib, w_gate[0], w_up[0], w_down[0]))
        came[step] = sibling(out[step][1])

    def merge_cores(step):
        total[step] = in_turn(add(out[step][0], came[step]).astype(BF16))
        other[step] = second(total[step][2 * my_rows :])

    def merge_second(step):
        kept[step] = in_turn(add(total[step][: 2 * my_rows], other[step]).astype(BF16))
        one[step] = first(kept[step][my_rows:])

    def merge_first(step):
        value = in_turn(add(kept[step][:my_rows], one[step]).astype(BF16))
        home[step] = returns[step](value)

    schedule = [
        (spread, 0, True),
        (spread, 1, True),
        (widen, 0, True),
        (spread, 2, True),
        (widen, 1, False),
        (share, 0, True),
        (spread, 3, True),
        (widen, 2, True),
        (widen, 3, False),
        (share, 1, True),
        (run, 1, True),
        (share, 2, True),
        (run, 2, True),
        (share, 3, True),
        (run, 3, True),
        (merge_cores, 1, False),
        (merge_second, 1, False),
        (run, 0, True),
        (merge_cores, 2, False),
        (merge_second, 2, False),
        (merge_first, 2, False),
        (merge_cores, 3, False),
        (merge_first, 1, True),
        (merge_second, 3, False),
        (merge_first, 3, False),
        (merge_cores, 0, True),
        (merge_second, 0, True),
    ]
    for take, step, tie in schedule:
        tied[0] = tie
        take(step)
    return add(hidden, kept[0][:my_rows], one[0], *(home[step] for step in range(1, planes))).astype(BF16)


def exchanged_plan(ep_count, attn_out, resid, norm_gain, expert_ids, gate_vals, w_gate, w_up, w_down):
    hidden_f32, normed = norm_rows(attn_out, resid, norm_gain)
    normed_all = lax.all_gather(normed, "tp", axis=0, tiled=True)
    tok_block, width = normed_all.shape
    capacity = 4 * tok_block * expert_ids.shape[1] // (3 * ep_count)
    flat_ids = expert_ids.reshape(-1)
    onehot = (flat_ids[:, None] == jnp.arange(ep_count, dtype=jnp.int32)[None, :]).astype(jnp.int32)
    rank_in = jnp.sum(onehot * (jnp.cumsum(onehot, axis=0) - onehot), axis=1)
    slot_index = (flat_ids * capacity + rank_in).reshape(tok_block, -1)
    slot_range = jnp.arange(ep_count * capacity, dtype=jnp.int32)
    hit = slot_index[None, :, :] == slot_range[:, None, None]
    placing = jnp.any(hit, axis=-1).astype(BF16)
    send_rows = jnp.dot(placing, normed_all, preferred_element_type=F32).astype(BF16)
    send_rows = send_rows.reshape(ep_count, capacity, width)
    received = lax.all_to_all(send_rows, "ep", split_axis=0, concat_axis=0, tiled=True)
    out_rows = expert_rows(received.reshape(-1, width), w_gate[0], w_up[0], w_down[0]).astype(BF16)
    back_rows = lax.all_to_all(
        out_rows.reshape(received.shape), "ep", split_axis=0, concat_axis=0, tiled=True
    )
    scale = jnp.sum(jnp.where(hit, gate_vals[None, :, :], 0.0), axis=(1, 2))
    weighted = (back_rows.reshape(-1, width).astype(F32) * scale[:, None]).astype(BF16)
    part = lax.dot_general(placing, weighted, (((0,), (0,)), ((), ())), preferred_element_type=F32)
    moe_rows = lax.psum_scatter(part, "tp", scatter_dimension=0, tiled=True)
    return (hidden_f32 + moe_rows).astype(BF16)


def solution(mesh):
    ep_count, tp_count = mesh.shape["ep"], mesh.shape["tp"]
    paired = tp_count == 2 and divmod(ep_count, 4) == (4, 0)
    plan = gathered_plan if paired else exchanged_plan

    def per_device(*arguments):
        return plan(ep_count, *arguments)

    in_specs = (
        P("ep", "tp"),
        P(AXES, None),
        P(),
        P("ep", None),
        P("ep", None),
        P("ep", "tp", None),
        P("ep", "tp", None),
        P("ep", "tp", None),
    )
    return jax.shard_map(
        per_device, mesh=mesh, in_specs=in_specs, out_specs=P(AXES, None), check_vma=False
    )
```
